512 devices in a mesh: head: 4 (over y), seq: 16 (over z_lo, x), tp: 8 (over z_hi, core).
Axes of the slice: x: 4, y: 4, z: 16 (z_hi: 4, z_lo: 4; z = z_hi * 4 + z_lo), core: 2. Of those that a mesh axis runs over, the one named last changes fastest.
Arguments:
- queries: bfloat16 [4, 3072, 64, 128], P('head', 'seq', 'tp'), may hold values from -4.75 to 4.75
- keys: bfloat16 [3072, 8, 128], P(('seq', 'tp')), may hold values from -4.75 to 4.75
- values: bfloat16 [3072, 8, 128], P(('seq', 'tp')), may hold values from -4 to 4
- doc_ids: int32 [3072], P('seq'), may hold values from 0 to 3, never falling along the last dimension, each value on 1 to 1536 neighbouring positions
- output_gradient: bfloat16 [4, 3072, 64, 128], P('head', 'seq', 'tp'), may hold values from -6 to 6
- attention_output: bfloat16 [4, 3072, 64, 128], P('head', 'seq', 'tp'), may hold values from -4 to 4
Outputs:
- grad_queries: bfloat16 [4, 3072, 64, 128], P('head', 'seq', 'tp')
- grad_keys: bfloat16 [3072, 8, 128], P(('head', 'seq'), 'tp')
- grad_values: bfloat16 [3072, 8, 128], P(('head', 'seq'), 'tp')
The draws below stay inside these ranges and needn't reach their ends.
Inputs may be any that keep to these rules, and one draw needn't show every extreme that they name: doc_ids never falls along the sequence; equal ids mark one packed document, the longest of 1536 positions.
All inputs are finite; a program needn't handle non-finite values.
Results may differ from the reference program's by a relative error of at most 0.006.
Values may be sent and summed in bfloat16 or wider, within the bound.
No kernel may reach another device: no remote copies, remote signals or barrier semaphores. Data moves between devices by JAX's collectives and lax.ppermute only.
A program may use at most 64 MiB of HBM per device.

```python
import math
import jax
import jax.numpy as jnp
import numpy as np
from jax import lax

QUERY_HEADS = 64
KEY_VALUE_HEADS = 8
HEAD_SIZE = 128
PREDICT_LAYERS = 4
SEQUENCE_LENGTH = 3072


def draw_keys(key, part):
    key = jax.random.fold_in(key, 1)
    base_offset = jnp.clip(jax.random.normal(key, (SEQUENCE_LENGTH, KEY_VALUE_HEADS, HEAD_SIZE), jnp.float32), -4.0, 4.0)
    return base_offset.astype(jnp.bfloat16)


def draw_queries(key, part):
    key = jax.random.fold_in(key, 2)
    base_offset = jnp.clip(jax.random.normal(key, (PREDICT_LAYERS, SEQUENCE_LENGTH, QUERY_HEADS, HEAD_SIZE), jnp.float32), -4.0, 4.0)
    return base_offset.astype(jnp.bfloat16)


def block_levels(rng, shape, shards, least, top_value):
    def one(dim, shards_of):
        draws = jax.random.uniform(jax.random.fold_in(jax.random.fold_in(rng, 6), dim), (shards_of,), jnp.float32, least / len(shards), top_value / len(shards))
        return jnp.repeat(jnp.exp(draws), shape[dim] // shards_of).reshape((-1,) + (1,) * (len(shape) - dim - 1))

    level = one(*shards[0])
    for cut in shards[1:]:
        level = level * one(*cut)
    return level


def profile(amount, total, bound, lean):
    weights = [(1 << 20) // math.isqrt(rank ** lean) + 1 for rank in range(2, amount + 1)]
    rest, counts = total - bound - (amount - 1), [1] * (amount - 1)
    while rest > 0:
        candidates = [i for i in range(amount - 1) if counts[i] < bound]
        mass, remaining = sum([weights[i] for i in candidates]), rest
        for i in candidates:
            addition = min(bound - counts[i], max(1, remaining * weights[i] // mass), rest)
            counts[i] = counts[i] + addition
            rest = rest - addition
    return np.array([bound] + counts)


def ragged_sizes(key, amount, total, most, skew):
    if amount == 2:
        one = jax.random.randint(key, (), max(1, total - most), min(most, total - 1) + 1)
        return jnp.stack([one, total - one])
    sizes = jnp.asarray(profile(amount, total, most, skew), jnp.int32)
    twos = (amount - 1) // 2
    source_of, receiver = sizes[1:1 + 2 * twos:2], sizes[2:2 + 2 * twos:2]
    margin = jnp.minimum(source_of - 1, most - receiver)
    shifted = jax.random.randint(jax.random.fold_in(key, 1), (twos,), 0, 1 << 20) % (margin + 1)
    sizes = sizes.at[1:1 + 2 * twos:2].set(source_of - shifted).at[2:2 + 2 * twos:2].set(receiver + shifted)
    return sizes[jax.random.permutation(jax.random.fold_in(key, 2), amount)]


def bell_draw(rng, dims, scale, most, cuts=(), held_as=jnp.bfloat16):
    values = scale * jax.random.normal(rng, dims, jnp.float32)
    if cuts:
        values = values * block_levels(rng, dims, cuts, -0.22, 0.18)
    return jnp.clip(values, -most, most).astype(held_as)


def setup_inputs(seed: int = 0) -> dict:
    splits = jax.random.split(jax.random.key(seed), 7)
    queries = draw_queries(jax.random.fold_in(splits[6], 71), 0)
    keys = draw_keys(jax.random.fold_in(splits[6], 71), 0)
    values = bell_draw(splits[2], (SEQUENCE_LENGTH, KEY_VALUE_HEADS, HEAD_SIZE), 1.0, 4.0, ((0, 128),))
    doc_ids = jnp.searchsorted(jnp.cumsum(ragged_sizes(splits[3], 4, SEQUENCE_LENGTH, SEQUENCE_LENGTH // 2, 0)), jnp.arange(SEQUENCE_LENGTH), side="right").astype(jnp.int32)
    output_gradient = bell_draw(splits[4], (PREDICT_LAYERS, SEQUENCE_LENGTH, QUERY_HEADS, HEAD_SIZE), 1.0, 6.0, ((0, 4), (1, 16), (2, 8)))
    attention_output = bell_draw(splits[5], (PREDICT_LAYERS, SEQUENCE_LENGTH, QUERY_HEADS, HEAD_SIZE), 1.0, 4.0, ((0, 4), (1, 16), (2, 8)))
    return dict(queries=queries, keys=keys, values=values, doc_ids=doc_ids, output_gradient=output_gradient, attention_output=attention_output)


def reference(queries, keys, values, doc_ids, output_gradient, attention_output):
    scale = HEAD_SIZE ** -0.5
    query_group = QUERY_HEADS // KEY_VALUE_HEADS
    positions = jnp.arange(SEQUENCE_LENGTH, dtype=jnp.int32)
    allowed = (doc_ids[:, None] == doc_ids[None, :]) & (positions[None, :] <= positions[:, None])
    allowed_rows = jnp.tile(allowed, (query_group, 1))
    query_reshaped = queries.reshape(PREDICT_LAYERS, SEQUENCE_LENGTH, KEY_VALUE_HEADS, query_group, HEAD_SIZE)
    gradient_reshaped = output_gradient.reshape(PREDICT_LAYERS, SEQUENCE_LENGTH, KEY_VALUE_HEADS, query_group, HEAD_SIZE)
    output_reshaped = attention_output.reshape(PREDICT_LAYERS, SEQUENCE_LENGTH, KEY_VALUE_HEADS, query_group, HEAD_SIZE)

    def head_slices(index):
        key_col = lax.dynamic_index_in_dim(keys, index, 1, keepdims=False)
        value_col = lax.dynamic_index_in_dim(values, index, 1, keepdims=False)
        query_sub = lax.dynamic_index_in_dim(query_reshaped, index, 2, keepdims=False)
        grad_sub = lax.dynamic_index_in_dim(gradient_reshaped, index, 2, keepdims=False)
        out_sub = lax.dynamic_index_in_dim(output_reshaped, index, 2, keepdims=False)
        key_total = jnp.zeros((SEQUENCE_LENGTH, HEAD_SIZE), jnp.float32)
        value_total = jnp.zeros((SEQUENCE_LENGTH, HEAD_SIZE), jnp.float32)
        query_parts = []
        for layer in range(PREDICT_LAYERS):
            rows = query_sub[layer].transpose(1, 0, 2).reshape(query_group * SEQUENCE_LENGTH, HEAD_SIZE)
            grad_rows = grad_sub[layer].transpose(1, 0, 2).reshape(query_group * SEQUENCE_LENGTH, HEAD_SIZE)
            out_rows = out_sub[layer].transpose(1, 0, 2).reshape(query_group * SEQUENCE_LENGTH, HEAD_SIZE)
            score = jnp.dot(rows, key_col.T, preferred_element_type=jnp.float32) * scale
            top = jnp.max(jnp.where(allowed_rows, score, -1e30), axis=1, keepdims=True)
            total = jnp.sum(jnp.where(allowed_rows, jnp.exp(score - top), 0.0), axis=1, keepdims=True)
            log_total = top + jnp.log(total)
            prob = jnp.where(allowed_rows, jnp.exp(score - log_total), 0.0)
            prob_low = prob.astype(jnp.bfloat16)
            delta = jnp.sum(grad_rows.astype(jnp.float32) * out_rows.astype(jnp.float32), axis=1, keepdims=True)
            prob_grad = jnp.dot(grad_rows, value_col.T, preferred_element_type=jnp.float32)
            score_grad = (prob * (prob_grad - delta)).astype(jnp.bfloat16)
            query_grad = jnp.dot(score_grad, key_col, preferred_element_type=jnp.float32) * scale
            query_parts.append(query_grad.astype(jnp.bfloat16).reshape(query_group, SEQUENCE_LENGTH, HEAD_SIZE))
            key_total = key_total + jnp.dot(score_grad.T, rows, preferred_element_type=jnp.float32) * scale
            value_total = value_total + jnp.dot(prob_low.T, grad_rows, preferred_element_type=jnp.float32)
        return jnp.stack(query_parts), key_total, value_total

    every_query, every_key, every_value = lax.map(head_slices, jnp.arange(KEY_VALUE_HEADS, dtype=jnp.int32))
    grad_queries = every_query.transpose(1, 3, 0, 2, 4).reshape(PREDICT_LAYERS, SEQUENCE_LENGTH, QUERY_HEADS, HEAD_SIZE)
    grad_keys = every_key.transpose(1, 0, 2).astype(jnp.bfloat16)
    grad_values = every_value.transpose(1, 0, 2).astype(jnp.bfloat16)
    return (grad_queries, grad_keys, grad_values)
```

```python
import functools
import jax
import jax.numpy as jnp
from jax import lax
from jax.experimental import pallas as pl
from jax.experimental.pallas import tpu as pltpu
from jax.sharding import PartitionSpec as P

F32, BF16 = jnp.float32, jnp.bfloat16
TOK = 192
BACK = 9
KB = 256
WIN = 1792
PAD = WIN - BACK * TOK
OWN = WIN - TOK
RT = 512
ROWS = 1536
HEADS = 8
LOG2E = 1.4426950408889634
NEG = -1e30
PAY = 208


def attention_kernel(
    where_ref, docs_ref, qdoc_ref, q_ref, do_ref, o_ref, own_ref, recv_ref,
    dq_ref, dkv_ref, kwin, vwin, dk_acc, dv_acc, t_scr,
):
    block = where_ref[0]
    x = lax.rem(block, 4)
    cnt = [jnp.zeros((1, 256), F32) for _ in range(3)]
    lane = lax.broadcasted_iota(jnp.int32, (1, 256), 1)
    kwin[0:PAD, :] = jnp.zeros((PAD, 128), BF16)
    vwin[0:PAD, :] = jnp.zeros((PAD, 128), BF16)
    for k in range(BACK):
        row = PAD + (BACK - 1 - k) * TOK
        if k % 4 == 0:
            src = own_ref.at[k // 4]
        else:
            src = recv_ref.at[lax.rem(x - k + 8, 4), k // 4]
        kwin[row:row + TOK, :] = src[0:TOK, 0:128]
        vwin[row:row + TOK, :] = src[0:TOK, 128:256]
        ids = src[TOK:TOK + 16, :].astype(F32)[0:1]
        ids = jnp.where(lane < TOK, ids, 100.0)
        for d in range(3):
            cnt[d] = cnt[d] + jnp.where(ids < d + 0.5, 1.0, 0.0)
    first_valid = OWN - block * TOK
    begin = [jnp.maximum(PAD, first_valid)]
    for d in range(3):
        begin.append(jnp.maximum(PAD + jnp.sum(cnt[d]).astype(jnp.int32), first_valid))

    def begin_of(doc):
        return jnp.where(
            doc == 0, begin[0], jnp.where(doc == 1, begin[1], jnp.where(doc == 2, begin[2], begin[3]))
        )

    dk_acc[...] = jnp.zeros_like(dk_acc)
    dv_acc[...] = jnp.zeros_like(dv_acc)
    c = (128.0 ** -0.5) * LOG2E
    tok_step = RT // HEADS
    last_kb = WIN // KB - 1

    def row_tile(i, unused):
        rows = pl.ds(pl.multiple_of(i * RT, RT), RT)
        q = q_ref[rows, :]
        do = do_ref[rows, :]
        delta = jnp.sum((do.astype(F32) * o_ref[rows, :].astype(F32)).T, axis=0, keepdims=True)
        start = begin_of(qdoc_ref[:, rows])
        tok = OWN + i * tok_step + lax.broadcasted_iota(jnp.int32, (1, RT), 1) // HEADS
        lo = begin_of(docs_ref[i * tok_step]) // KB
        mid = jnp.minimum((begin_of(docs_ref[i * tok_step + tok_step - 1]) + KB - 1) // KB, last_kb)

        def score_step(masked, kb, top):
            keys = pl.ds(pl.multiple_of(kb * KB, KB), KB)
            t = lax.dot_general(kwin[keys, :], q, (((1,), (1,)), ((), ())), preferred_element_type=F32) * c
            if masked:
                kp = kb * KB + lax.broadcasted_iota(jnp.int32, (KB, RT), 0)
                t = jnp.where((kp >= start) & (kp <= tok), t, NEG)
            t_scr[keys, :] = t
            return jnp.maximum(top, jnp.max(t.reshape(KB // 8, 8, RT), axis=0))

        top = jnp.full((8, RT), NEG, F32)
        top = lax.fori_loop(lo, mid, functools.partial(score_step, True), top)
        top = lax.fori_loop(mid, last_kb, functools.partial(score_step, False), top)
        top = score_step(True, last_kb, top)
        top = jnp.max(top, axis=0, keepdims=True)

        def exp_step(kb, total):
            keys = pl.ds(pl.multiple_of(kb * KB, KB), KB)
            e = jnp.exp2(t_scr[keys, :] - top)
            t_scr[keys, :] = e
            return total + jnp.sum(e.reshape(KB // 8, 8, RT), axis=0)

        total = lax.fori_loop(lo, last_kb + 1, exp_step, jnp.zeros((8, RT), F32))
        inv = 1.0 / jnp.sum(total, axis=0, keepdims=True)

        def grad_step(kb, dq):
            keys = pl.ds(pl.multiple_of(kb * KB, KB), KB)
            prob = t_scr[keys, :] * inv
            dp = lax.dot_general(vwin[keys, :], do, (((1,), (1,)), ((), ())), preferred_element_type=F32)
            ds = (prob * (dp - delta)).astype(BF16)
            dv_acc[keys, :] += jnp.dot(prob.astype(BF16), do, preferred_element_type=F32)
            dk_acc[keys, :] += jnp.dot(ds, q, preferred_element_type=F32)
            return dq + lax.dot_general(ds, kwin[keys, :], (((0,), (0,)), ((), ())), preferred_element_type=F32)

        dq = lax.fori_loop(lo, last_kb + 1, grad_step, jnp.zeros((RT, 128), F32))
        dq_ref[rows, :] = (dq * (128.0 ** -0.5)).astype(BF16)
        return unused

    lax.fori_loop(0, ROWS // RT, row_tile, 0)
    for k in range(BACK):
        row = PAD + (BACK - 1 - k) * TOK
        for r in range(4):
            part = slice(row + r * 48, row + r * 48 + 48)
            dkv_ref[r, k, :, 0:128] = dk_acc[part, :].astype(BF16)
            dkv_ref[r, k, :, 128:256] = dv_acc[part, :].astype(BF16)


def attention_grads(where, docs, qdoc, q, do, o, own, recv):
    vmem = pl.BlockSpec(memory_space=pltpu.VMEM)
    smem = pl.BlockSpec(memory_space=pltpu.SMEM)
    return pl.pallas_call(
        attention_kernel,
        out_shape=(
            jax.ShapeDtypeStruct((ROWS, 128), BF16),
            jax.ShapeDtypeStruct((4, BACK, 48, 256), BF16),
        ),
        in_specs=[smem, smem, vmem, vmem, vmem, vmem, vmem, vmem],
        out_specs=(vmem, vmem),
        scratch_shapes=[
            pltpu.VMEM((WIN, 128), BF16),
            pltpu.VMEM((WIN, 128), BF16),
            pltpu.VMEM((WIN, 128), F32),
            pltpu.VMEM((WIN, 128), F32),
            pltpu.VMEM((WIN, RT), F32),
        ],
        compiler_params=pltpu.CompilerParams(vmem_limit_bytes=40 << 20),
        cost_estimate=pl.CostEstimate(flops=3 << 30, bytes_accessed=3 << 20, transcendentals=2 << 20),
    )(where, docs, qdoc, q, do, o, own, recv)


X_GROUPS = [[4 * a + x for x in range(4)] for a in range(4)]


def on_device(queries, keys, values, doc_ids, output_gradient, attention_output):
    block = lax.axis_index("seq")
    a, x = block // 4, lax.rem(block, 4)
    kv = jnp.concatenate([keys, values], axis=2).transpose(1, 0, 2)
    kv = lax.all_to_all(kv, "tp", split_axis=0, concat_axis=0, tiled=True).reshape(TOK, 256)
    ids = jnp.pad(doc_ids.astype(BF16), (0, 64))
    tail = jnp.concatenate([ids[None], jnp.zeros((PAY - TOK - 1, 256), BF16)], axis=0)
    pay = jnp.concatenate([kv, tail], axis=0)
    back = [lax.ppermute(pay, "seq", [(i, i + k) for i in range(16 - k)]) for k in (4, 8)]
    own = jnp.stack([pay] + back)
    send = jnp.stack([jnp.where(x < dest, own[0:2], own[1:3]) for dest in range(4)])
    recv = lax.all_to_all(send, "seq", split_axis=0, concat_axis=0, tiled=True, axis_index_groups=X_GROUPS)
    qdoc = jnp.repeat(doc_ids, HEADS)[None]
    dq, dkv = attention_grads(
        block.reshape(1), doc_ids, qdoc,
        queries.reshape(ROWS, 128), output_gradient.reshape(ROWS, 128), attention_output.reshape(ROWS, 128),
        own, recv,
    )
    part = lax.all_to_all(dkv, "seq", split_axis=0, concat_axis=0, tiled=True, axis_index_groups=X_GROUPS)
    part = part.astype(F32)
    slots = []
    for j in range(12):
        terms = [part[xs, 8 + xs - j] for xs in range(4) if 0 <= 8 + xs - j < BACK]
        slots.append(sum(terms[1:], terms[0]))
    summed = jnp.stack(slots).astype(BF16).reshape(3, 4, 48, 256)
    wide = lax.dynamic_update_slice(jnp.zeros((6, 4, 48, 256), BF16), summed, (a, 0, 0, 0))[2:]
    wide = lax.all_to_all(wide, "head", split_axis=0, concat_axis=0, tiled=True)
    wide = jnp.sum(wide.astype(F32), axis=0).astype(BF16)
    z_groups = [[4 * i + j for i in range(4)] for j in range(4)]
    last = lax.all_to_all(wide, "seq", split_axis=0, concat_axis=0, tiled=True, axis_index_groups=z_groups)
    last = jnp.sum(last.astype(F32), axis=0)
    grad_keys = (last[:, 0:128] * (128.0 ** -0.5)).astype(BF16)[:, None]
    grad_values = last[:, 128:256].astype(BF16)[:, None]
    return dq.reshape(1, TOK, HEADS, 128), grad_keys, grad_values


def solution(mesh):
    placed = (
        P("head", "seq", "tp", None),
        P(("seq", "tp"), None, None),
        P(("seq", "tp"), None, None),
        P("seq"),
        P("head", "seq", "tp", None),
        P("head", "seq", "tp", None),
    )
    return jax.shard_map(
        on_device,
        mesh=mesh,
        in_specs=placed,
        out_specs=(
            P("head", "seq", "tp", None),
            P(("head", "seq"), "tp", None),
            P(("head", "seq"), "tp", None),
        ),
        check_vma=False,
    )
```

```python
import functools
import jax
import jax.numpy as jnp
from jax import lax
from jax.experimental import pallas as pl
from jax.experimental.pallas import tpu as pltpu
from jax.sharding import PartitionSpec as P

F32, BF16 = jnp.float32, jnp.bfloat16
TOK = 192
BACK = 9
KB = 576
LAST = BACK * TOK // KB - 1
ROWS = 1536
HEADS = 8
LOG2E = 1.4426950408889634
NEG = -1e30
SCALE2 = (128.0 ** -0.5) * LOG2E
OWN = (BACK - 1) * TOK
PAY = 208
NT = (((1,), (1,)), ((), ()))
TN = (((0,), (0,)), ((), ()))


def keys_of(k):
    return pl.ds(pl.multiple_of(k * KB, KB), KB)


def load_window(where_ref, own_ref, recv_ref, kwin, vwin):
    block = where_ref[0]
    x = lax.rem(block, 4)
    cnt = [jnp.zeros((1, 256), F32) for _ in range(3)]
    lane = lax.broadcasted_iota(jnp.int32, (1, 256), 1)
    for k in range(BACK):
        if k % 4 == 0:
            src = own_ref.at[k // 4]
        else:
            src = recv_ref.at[lax.rem(x - k + 8, 4), k // 4]
        place = slice((BACK - 1 - k) * TOK, (BACK - k) * TOK)
        kwin[place, :] = src[0:TOK, 0:128]
        vwin[place, :] = src[0:TOK, 128:256]
        ids = src[TOK:TOK + 16, :].astype(F32)[0:1]
        ids = jnp.where(lane < TOK, ids, 100.0)
        for d in range(3):
            cnt[d] = cnt[d] + jnp.where(ids < d + 0.5, 1.0, 0.0)
    first_valid = jnp.maximum(OWN - block * TOK, 0)
    begin = [first_valid]
    for d in range(3):
        begin.append(jnp.maximum(jnp.sum(cnt[d]).astype(jnp.int32), first_valid))
    return begin


def begin_of(begin, doc):
    return jnp.where(
        doc == 0, begin[0], jnp.where(doc == 1, begin[1], jnp.where(doc == 2, begin[2], begin[3]))
    )


def scaled_scores(key, q, start, k, masked, own):
    t = lax.dot_general(key, q, NT, preferred_element_type=F32) * SCALE2
    if masked or own:
        kp = lax.broadcasted_iota(jnp.int32, (KB, ROWS), 0)
        allowed = kp >= start - k * KB
        if own:
            tok = OWN - LAST * KB + lax.broadcasted_iota(jnp.int32, (1, ROWS), 1) // HEADS
            allowed = allowed & (kp <= tok)
        t = jnp.where(allowed, t, NEG)
    return t


def over_window(step, low, mid):
    lax.fori_loop(low, mid, functools.partial(step, masked=True, own=False), 0)
    lax.fori_loop(mid, LAST, functools.partial(step, masked=False, own=False), 0)
    step(LAST, 0, True, True)


def key_value_kernel(
    where_ref, docs_ref, qdoc_ref, q_ref, do_ref, o_ref, own_ref, recv_ref,
    dkv_ref, stat_ref, kwin, vwin, t_scr, m_scr, l_scr, start_scr,
):
    begin = load_window(where_ref, own_ref, recv_ref, kwin, vwin)
    start_scr[...] = begin_of(begin, qdoc_ref[...])
    low = begin_of(begin, docs_ref[0]) // KB
    mid = jnp.minimum((begin_of(begin, docs_ref[TOK - 1]) + KB - 1) // KB, LAST)
    m_scr[...] = jnp.full_like(m_scr, NEG)
    l_scr[...] = jnp.zeros_like(l_scr)

    def score_step(k, unused, masked, own):
        t = scaled_scores(kwin[keys_of(k), :], q_ref[...], start_scr[...], k, masked, own)
        t_scr[keys_of(k), :] = t
        t = t.reshape(KB // 8, 8, ROWS)
        old = m_scr[...]
        top = jnp.maximum(old, jnp.max(t, axis=0))
        m_scr[...] = top
        l_scr[...] = l_scr[...] * jnp.exp2(old - top) + jnp.sum(jnp.exp2(t - top), axis=0)
        return unused

    over_window(score_step, low, mid)
    top = jnp.max(m_scr[...], axis=0, keepdims=True)
    total = jnp.sum(l_scr[...] * jnp.exp2(m_scr[...] - top), axis=0, keepdims=True)
    stat_ref[0:1, :] = top + jnp.log(total) * LOG2E
    stat_ref[1:2, :] = jnp.sum((do_ref[...].astype(F32) * o_ref[...].astype(F32)).T, axis=0, keepdims=True)

    def grad_step(k, unused):
        q, do = q_ref[...], do_ref[...]
        prob = jnp.exp2(t_scr[keys_of(k), :] - stat_ref[0:1, :])
        dp = lax.dot_general(vwin[keys_of(k), :], do, NT, preferred_element_type=F32)
        ds = (prob * (dp - stat_ref[1:2, :])).astype(BF16)
        dv = jnp.dot(prob.astype(BF16), do, preferred_element_type=F32)
        dk = jnp.dot(ds, q, preferred_element_type=F32)
        for b in range(KB // TOK):
            for r in range(4):
                part = slice(b * TOK + r * 48, b * TOK + r * 48 + 48)
                back = BACK - 1 - b - k * (KB // TOK)
                dkv_ref[r, back, :, 0:128] = dk[part].astype(BF16)
                dkv_ref[r, back, :, 128:256] = dv[part].astype(BF16)
        return unused

    lax.fori_loop(low, LAST + 1, grad_step, 0)

    def clear_step(k, unused):
        for b in range(KB // TOK):
            for r in range(4):
                dkv_ref[r, BACK - 1 - b - k * (KB // TOK)] = jnp.zeros((48, 256), BF16)
        return unused

    lax.fori_loop(0, low, clear_step, 0)


def query_kernel(
    where_ref, docs_ref, qdoc_ref, q_ref, do_ref, stat_ref, own_ref, recv_ref,
    dq_ref, kwin, vwin, dq_acc, start_scr,
):
    begin = load_window(where_ref, own_ref, recv_ref, kwin, vwin)
    start_scr[...] = begin_of(begin, qdoc_ref[...])
    low = begin_of(begin, docs_ref[0]) // KB
    mid = jnp.minimum((begin_of(begin, docs_ref[TOK - 1]) + KB - 1) // KB, LAST)
    dq_acc[...] = jnp.zeros_like(dq_acc)

    def query_step(k, unused, masked, own):
        key = kwin[keys_of(k), :]
        t = scaled_scores(key, q_ref[...], start_scr[...], k, masked, own)
        prob = jnp.exp2(t - stat_ref[0:1, :])
        dp = lax.dot_general(vwin[keys_of(k), :], do_ref[...], NT, preferred_element_type=F32)
        ds = (prob * (dp - stat_ref[1:2, :])).astype(BF16)
        dq_acc[...] += lax.dot_general(key, ds, TN, preferred_element_type=F32)
        return unused

    over_window(query_step, low, mid)
    dq_ref[...] = (dq_acc[...].T * (128.0 ** -0.5)).astype(BF16)


VMEM_SPEC = pl.BlockSpec(memory_space=pltpu.VMEM)
SMEM_SPEC = pl.BlockSpec(memory_space=pltpu.SMEM)


def key_value_grads(where, docs, qdoc, q, do, o, own, recv):
    return pl.pallas_call(
        key_value_kernel,
        out_shape=(
            jax.ShapeDtypeStruct((4, BACK, 48, 256), BF16),
            jax.ShapeDtypeStruct((8, ROWS), F32),
        ),
        in_specs=[SMEM_SPEC, SMEM_SPEC] + [VMEM_SPEC] * 6,
        out_specs=(VMEM_SPEC, VMEM_SPEC),
        scratch_shapes=[
            pltpu.VMEM((BACK * TOK, 128), BF16),
            pltpu.VMEM((BACK * TOK, 128), BF16),
            pltpu.VMEM((BACK * TOK, ROWS), F32),
            pltpu.VMEM((8, ROWS), F32),
            pltpu.VMEM((8, ROWS), F32),
            pltpu.VMEM((1, ROWS), jnp.int32),
        ],
        compiler_params=pltpu.CompilerParams(vmem_limit_bytes=40 << 20),
        cost_estimate=pl.CostEstimate(flops=4 << 30, bytes_accessed=3 << 20, transcendentals=2 << 20),
    )(where, docs, qdoc, q, do, o, own, recv)


def query_grads(where, docs, qdoc, q, do, stat, own, recv):
    return pl.pallas_call(
        query_kernel,
        out_shape=jax.ShapeDtypeStruct((ROWS, 128), BF16),
        in_specs=[SMEM_SPEC, SMEM_SPEC] + [VMEM_SPEC] * 6,
        out_specs=VMEM_SPEC,
        scratch_shapes=[
            pltpu.VMEM((BACK * TOK, 128), BF16),
            pltpu.VMEM((BACK * TOK, 128), BF16),
            pltpu.VMEM((128, ROWS), F32),
            pltpu.VMEM((1, ROWS), jnp.int32),
        ],
        compiler_params=pltpu.CompilerParams(vmem_limit_bytes=40 << 20),
        cost_estimate=pl.CostEstimate(flops=3 << 30, bytes_accessed=3 << 20, transcendentals=2 << 20),
    )(where, docs, qdoc, q, do, stat, own, recv)


def attention_grads(where, docs, qdoc, q, do, o, own, recv):
    dkv, stat = key_value_grads(where, docs, qdoc, q, do, o, own, recv)
    return query_grads(where, docs, qdoc, q, do, stat, own, recv), dkv


X_GROUPS = [[4 * a + x for x in range(4)] for a in range(4)]


def on_device(queries, keys, values, doc_ids, output_gradient, attention_output):
    block = lax.axis_index("seq")
    a, x = block // 4, lax.rem(block, 4)
    kv = jnp.concatenate([keys, values], axis=2).transpose(1, 0, 2)
    kv = lax.all_to_all(kv, "tp", split_axis=0, concat_axis=0, tiled=True).reshape(TOK, 256)
    ids = jnp.pad(doc_ids.astype(BF16), (0, 64))
    tail = jnp.concatenate([ids[None], jnp.zeros((PAY - TOK - 1, 256), BF16)], axis=0)
    pay = jnp.concatenate([kv, tail], axis=0)
    back = [lax.ppermute(pay, "seq", [(i, i + k) for i in range(16 - k)]) for k in (4, 8)]
    own = jnp.stack([pay] + back)
    send = jnp.stack([jnp.where(x < dest, own[0:2], own[1:3]) for dest in range(4)])
    recv = lax.all_to_all(send, "seq", split_axis=0, concat_axis=0, tiled=True, axis_index_groups=X_GROUPS)
    qdoc = jnp.repeat(doc_ids, HEADS)[None]
    dq, dkv = attention_grads(
        block.reshape(1), doc_ids, qdoc,
        queries.reshape(ROWS, 128), output_gradient.reshape(ROWS, 128), attention_output.reshape(ROWS, 128),
        own, recv,
    )
    part = lax.all_to_all(dkv, "seq", split_axis=0, concat_axis=0, tiled=True, axis_index_groups=X_GROUPS)
    part, dq = lax.optimization_barrier((part, dq))
    part = part.astype(F32)
    slots = []
    for j in range(12):
        terms = [part[xs, 8 + xs - j] for xs in range(4) if 0 <= 8 + xs - j < BACK]
        slots.append(sum(terms[1:], terms[0]))
    summed = jnp.stack(slots).astype(BF16).reshape(3, 4, 48, 256)
    wide = lax.dynamic_update_slice(jnp.zeros((6, 4, 48, 256), BF16), summed, (a, 0, 0, 0))[2:]
    last = lax.all_to_all(
        wide.reshape(16, 48, 256), ("head", "seq"), split_axis=0, concat_axis=0, tiled=True,
        axis_index_groups=[[16 * h + 4 * z + xs for h in range(4) for z in range(4)] for xs in range(4)],
    )
    last = jnp.sum(last.astype(F32), axis=0)
    grad_keys = (last[:, 0:128] * (128.0 ** -0.5)).astype(BF16)[:, None]
    grad_values = last[:, 128:256].astype(BF16)[:, None]
    return dq.reshape(1, TOK, HEADS, 128), grad_keys, grad_values


def solution(mesh):
    placed = (
        P("head", "seq", "tp", None),
        P(("seq", "tp"), None, None),
        P(("seq", "tp"), None, None),
        P("seq"),
        P("head", "seq", "tp", None),
        P("head", "seq", "tp", None),
    )
    return jax.shard_map(
        on_device,
        mesh=mesh,
        in_specs=placed,
        out_specs=(
            P("head", "seq", "tp", None),
            P(("head", "seq"), "tp", None),
            P(("head", "seq"), "tp", None),
        ),
        check_vma=False,
    )
```

```python
import functools
import jax
import jax.numpy as jnp
from jax import lax
from jax.experimental import pallas as pl
from jax.experimental.pallas import tpu as pltpu
from jax.sharding import PartitionSpec as P

F32, BF16 = jnp.float32, jnp.bfloat16
TOK = 192
BACK = 9
KB = 576
LAST = BACK * TOK // KB - 1
ROWS = 1536
HEADS = 8
LOG2E = 1.4426950408889634
NEG = -1e30
SCALE2 = (128.0 ** -0.5) * LOG2E
OWN = (BACK - 1) * TOK
PAY = 200
NT = (((1,), (1,)), ((), ()))
TN = (((0,), (0,)), ((), ()))


def keys_of(k):
    return pl.ds(pl.multiple_of(k * KB, KB), KB)


def load_window(where_ref, own_ref, recv_ref, kwin, vwin):
    block = where_ref[0]
    x = lax.rem(block, 4)
    cnt = [jnp.zeros((1, 256), F32) for _ in range(3)]
    lane = lax.broadcasted_iota(jnp.int32, (1, 256), 1)
    for k in range(BACK):
        if k % 4 == 0:
            src = own_ref.at[k // 4]
        else:
            src = recv_ref.at[lax.rem(x - k + 8, 4), k // 4]
        place = slice((BACK - 1 - k) * TOK, (BACK - k) * TOK)
        kwin[place, :] = src[0:TOK, 0:128]
        vwin[place, :] = src[0:TOK, 128:256]
        ids = src[TOK:TOK + 8, :].astype(F32)[0:1]
        ids = jnp.where(lane < TOK, ids, 100.0)
        for d in range(3):
            cnt[d] = cnt[d] + jnp.where(ids < d + 0.5, 1.0, 0.0)
    first_valid = jnp.maximum(OWN - block * TOK, 0)
    begin = [first_valid]
    for d in range(3):
        begin.append(jnp.maximum(jnp.sum(cnt[d]).astype(jnp.int32), first_valid))
    return begin


def begin_of(begin, doc):
    return jnp.where(
        doc == 0, begin[0], jnp.where(doc == 1, begin[1], jnp.where(doc == 2, begin[2], begin[3]))
    )


def scaled_scores(key, q, start, k, masked, own):
    t = lax.dot_general(key, q, NT, preferred_element_type=F32) * SCALE2
    if masked or own:
        kp = lax.broadcasted_iota(jnp.int32, (KB, ROWS), 0)
        allowed = kp >= start - k * KB
        if own:
            tok = OWN - LAST * KB + lax.broadcasted_iota(jnp.int32, (1, ROWS), 1) // HEADS
            allowed = allowed & (kp <= tok)
        t = jnp.where(allowed, t, NEG)
    return t


def over_window(step, low, mid):
    lax.fori_loop(low, mid, functools.partial(step, masked=True, own=False), 0)
    lax.fori_loop(mid, LAST, functools.partial(step, masked=False, own=False), 0)
    step(LAST, 0, True, True)


def key_value_kernel(
    where_ref, docs_ref, qdoc_ref, q_ref, do_ref, o_ref, own_ref, recv_ref,
    dkv_ref, stat_ref, kwin, vwin, t_scr, m_scr, l_scr, start_scr,
):
    begin = load_window(where_ref, own_ref, recv_ref, kwin, vwin)
    start_scr[...] = begin_of(begin, qdoc_ref[...])
    low = begin_of(begin, docs_ref[0]) // KB
    mid = jnp.minimum((begin_of(begin, docs_ref[TOK - 1]) + KB - 1) // KB, LAST)
    m_scr[...] = jnp.full_like(m_scr, NEG)
    l_scr[...] = jnp.zeros_like(l_scr)

    def score_step(k, unused, masked, own):
        t = scaled_scores(kwin[keys_of(k), :], q_ref[...], start_scr[...], k, masked, own)
        t_scr[keys_of(k), :] = t
        t = t.reshape(KB // 8, 8, ROWS)
        old = m_scr[...]
        top = jnp.maximum(old, jnp.max(t, axis=0))
        m_scr[...] = top
        l_scr[...] = l_scr[...] * jnp.exp2(old - top) + jnp.sum(jnp.exp2(t - top), axis=0)
        return unused

    over_window(score_step, low, mid)
    top = jnp.max(m_scr[...], axis=0, keepdims=True)
    total = jnp.sum(l_scr[...] * jnp.exp2(m_scr[...] - top), axis=0, keepdims=True)
    stat_ref[0:1, :] = top + jnp.log(total) * LOG2E
    stat_ref[1:2, :] = jnp.sum((do_ref[...].astype(F32) * o_ref[...].astype(F32)).T, axis=0, keepdims=True)

    def grad_step(k, unused):
        q, do = q_ref[...], do_ref[...]
        prob = jnp.exp2(t_scr[keys_of(k), :] - stat_ref[0:1, :])
        dp = lax.dot_general(vwin[keys_of(k), :], do, NT, preferred_element_type=F32)
        ds = (prob * (dp - stat_ref[1:2, :])).astype(BF16)
        dv = jnp.dot(prob.astype(BF16), do, preferred_element_type=F32)
        dk = jnp.dot(ds, q, preferred_element_type=F32)
        for b in range(KB // TOK):
            for r in range(4):
                part = slice(b * TOK + r * 48, b * TOK + r * 48 + 48)
                back = BACK - 1 - b - k * (KB // TOK)
                dkv_ref[r, back, :, 0:128] = dk[part].astype(BF16)
                dkv_ref[r, back, :, 128:256] = dv[part].astype(BF16)
        return unused

    lax.fori_loop(low, LAST + 1, grad_step, 0)

    def clear_step(k, unused):
        for b in range(KB // TOK):
            for r in range(4):
                dkv_ref[r, BACK - 1 - b - k * (KB // TOK)] = jnp.zeros((48, 256), BF16)
        return unused

    lax.fori_loop(0, low, clear_step, 0)


def query_kernel(
    where_ref, docs_ref, qdoc_ref, q_ref, do_ref, stat_ref, own_ref, recv_ref,
    dq_ref, kwin, vwin, dq_acc, start_scr,
):
    begin = load_window(where_ref, own_ref, recv_ref, kwin, vwin)
    start_scr[...] = begin_of(begin, qdoc_ref[...])
    low = begin_of(begin, docs_ref[0]) // KB
    mid = jnp.minimum((begin_of(begin, docs_ref[TOK - 1]) + KB - 1) // KB, LAST)
    dq_acc[...] = jnp.zeros_like(dq_acc)

    def query_step(k, unused, masked, own):
        key = kwin[keys_of(k), :]
        t = scaled_scores(key, q_ref[...], start_scr[...], k, masked, own)
        prob = jnp.exp2(t - stat_ref[0:1, :])
        dp = lax.dot_general(vwin[keys_of(k), :], do_ref[...], NT, preferred_element_type=F32)
        ds = (prob * (dp - stat_ref[1:2, :])).astype(BF16)
        dq_acc[...] += lax.dot_general(key, ds, TN, preferred_element_type=F32)
        return unused

    over_window(query_step, low, mid)
    dq_ref[...] = (dq_acc[...].T * (128.0 ** -0.5)).astype(BF16)


VMEM_SPEC = pl.BlockSpec(memory_space=pltpu.VMEM)
SMEM_SPEC = pl.BlockSpec(memory_space=pltpu.SMEM)


def key_value_grads(where, docs, qdoc, q, do, o, own, recv):
    return pl.pallas_call(
        key_value_kernel,
        out_shape=(
            jax.ShapeDtypeStruct((4, BACK, 48, 256), BF16),
            jax.ShapeDtypeStruct((8, ROWS), F32),
        ),
        in_specs=[SMEM_SPEC, SMEM_SPEC] + [VMEM_SPEC] * 6,
        out_specs=(VMEM_SPEC, VMEM_SPEC),
        scratch_shapes=[
            pltpu.VMEM((BACK * TOK, 128), BF16),
            pltpu.VMEM((BACK * TOK, 128), BF16),
            pltpu.VMEM((BACK * TOK, ROWS), F32),
            pltpu.VMEM((8, ROWS), F32),
            pltpu.VMEM((8, ROWS), F32),
            pltpu.VMEM((1, ROWS), jnp.int32),
        ],
        compiler_params=pltpu.CompilerParams(vmem_limit_bytes=40 << 20),
        cost_estimate=pl.CostEstimate(flops=4 << 30, bytes_accessed=3 << 20, transcendentals=2 << 20),
    )(where, docs, qdoc, q, do, o, own, recv)


def query_grads(where, docs, qdoc, q, do, stat, own, recv):
    return pl.pallas_call(
        query_kernel,
        out_shape=jax.ShapeDtypeStruct((ROWS, 128), BF16),
        in_specs=[SMEM_SPEC, SMEM_SPEC] + [VMEM_SPEC] * 6,
        out_specs=VMEM_SPEC,
        scratch_shapes=[
            pltpu.VMEM((BACK * TOK, 128), BF16),
            pltpu.VMEM((BACK * TOK, 128), BF16),
            pltpu.VMEM((128, ROWS), F32),
            pltpu.VMEM((1, ROWS), jnp.int32),
        ],
        compiler_params=pltpu.CompilerParams(vmem_limit_bytes=40 << 20),
        cost_estimate=pl.CostEstimate(flops=3 << 30, bytes_accessed=3 << 20, transcendentals=2 << 20),
    )(where, docs, qdoc, q, do, stat, own, recv)


def attention_grads(where, docs, qdoc, q, do, o, own, recv):
    dkv, stat = key_value_grads(where, docs, qdoc, q, do, o, own, recv)
    return query_grads(where, docs, qdoc, q, do, stat, own, recv), dkv


def sum_kernel(group_ref, part_ref, out_ref):
    first = 4 * group_ref[0] - 8
    out_ref[...] = jnp.zeros_like(out_ref)
    for j in range(12):

        @pl.when(first + j >= 0)
        def _():
            terms = [part_ref[xs, 8 + xs - j].astype(F32) for xs in range(4) if 0 <= 8 + xs - j < BACK]
            out_ref[jnp.maximum(first + j, 0)] = sum(terms[1:], terms[0]).astype(BF16)


def sum_terms(group, part):
    return pl.pallas_call(
        sum_kernel,
        out_shape=jax.ShapeDtypeStruct((16, 48, 256), BF16),
        in_specs=[SMEM_SPEC, VMEM_SPEC],
        out_specs=VMEM_SPEC,
        compiler_params=pltpu.CompilerParams(vmem_limit_bytes=8 << 20),
        cost_estimate=pl.CostEstimate(flops=1 << 20, bytes_accessed=1 << 20, transcendentals=0),
    )(group, part)


def finish_kernel(last_ref, dk_ref, dv_ref):
    total = jnp.sum(last_ref[...].astype(F32), axis=0)
    dk_ref[...] = (total[:, 0:128] * (128.0 ** -0.5)).astype(BF16)
    dv_ref[...] = total[:, 128:256].astype(BF16)


def finish(last):
    return pl.pallas_call(
        finish_kernel,
        out_shape=(jax.ShapeDtypeStruct((48, 128), BF16),) * 2,
        in_specs=[VMEM_SPEC],
        out_specs=(VMEM_SPEC, VMEM_SPEC),
        compiler_params=pltpu.CompilerParams(vmem_limit_bytes=8 << 20),
        cost_estimate=pl.CostEstimate(flops=1 << 18, bytes_accessed=1 << 19, transcendentals=0),
    )(last)


X_GROUPS = [[4 * a + x for x in range(4)] for a in range(4)]


def on_device(queries, keys, values, doc_ids, output_gradient, attention_output):
    block = lax.axis_index("seq")
    a, x = block // 4, lax.rem(block, 4)
    tp = lax.axis_index("tp")
    core, half = tp % 2 == 1, tp >= 4
    near = ((tp // 2) % 2 == 1) != half
    bits = (half, near, core)

    def by_label(array):
        for axis, bit in enumerate(bits):
            array = jnp.where(bit, jnp.flip(array, axis), array)
        return array

    def relabel(array):
        return jnp.stack([array[0:2], jnp.flip(array[2:4], 0)])

    def by_core(array):
        return jnp.where(core, jnp.swapaxes(array, 0, 1), array)

    def swap(array, flip0, flip1):
        return lax.ppermute(array, "tp", [(i, i ^ (flip1 if i % 2 else flip0)) for i in range(8)])

    kv = jnp.concatenate([keys, values], axis=2).transpose(1, 0, 2).reshape(4, 2, 24, 256)
    part = by_label(relabel(kv))
    got = swap(part[:, :, 1], 1, 1)
    part = by_core(jnp.stack([part[:, :, 0], got], axis=2))
    got = swap(part[:, 1], 2, 6)
    part = jnp.stack([part[:, 0], got], axis=1)
    got = swap(part[1], 6, 2)
    part = by_label(by_core(jnp.stack([part[0], got])))
    kv = jnp.concatenate([part[0], jnp.flip(part[1], 0)]).reshape(TOK, 256)
    ids = jnp.pad(doc_ids.astype(BF16), (0, 64))
    tail = jnp.concatenate([ids[None], jnp.zeros((PAY - TOK - 1, 256), BF16)], axis=0)
    pay = jnp.concatenate([kv, tail], axis=0)
    back = [lax.ppermute(pay, "seq", [(i, i + k) for i in range(16 - k)]) for k in (4, 8)]
    own = jnp.stack([pay] + back)
    send = jnp.stack([jnp.where(x < dest, own[0:2], own[1:3]) for dest in range(4)])
    recv = lax.all_to_all(send, "seq", split_axis=0, concat_axis=0, tiled=True, axis_index_groups=X_GROUPS)
    qdoc = jnp.repeat(doc_ids, HEADS)[None]
    dq, dkv = attention_grads(
        block.reshape(1), doc_ids, qdoc,
        queries.reshape(ROWS, 128), output_gradient.reshape(ROWS, 128), attention_output.reshape(ROWS, 128),
        own, recv,
    )
    part = lax.all_to_all(dkv, "seq", split_axis=0, concat_axis=0, tiled=True, axis_index_groups=X_GROUPS)
    part, dq = lax.optimization_barrier((part, dq))
    last = lax.all_to_all(
        sum_terms(a.reshape(1), part), ("head", "seq"), split_axis=0, concat_axis=0, tiled=True,
        axis_index_groups=[[16 * h + 4 * z + xs for h in range(4) for z in range(4)] for xs in range(4)],
    )
    grad_keys, grad_values = finish(last)
    grad_keys, grad_values = grad_keys[:, None], grad_values[:, None]
    return dq.reshape(1, TOK, HEADS, 128), grad_keys, grad_values


def solution(mesh):
    placed = (
        P("head", "seq", "tp", None),
        P(("seq", "tp"), None, None),
        P(("seq", "tp"), None, None),
        P("seq"),
        P("head", "seq", "tp", None),
        P("head", "seq", "tp", None),
    )
    return jax.shard_map(
        on_device,
        mesh=mesh,
        in_specs=placed,
        out_specs=(
            P("head", "seq", "tp", None),
            P(("head", "seq"), "tp", None),
            P(("head", "seq"), "tp", None),
        ),
        check_vma=False,
    )
```

```python
import functools
import jax
import jax.numpy as jnp
from jax import lax
from jax.experimental import pallas as pl
from jax.experimental.pallas import tpu as pltpu
from jax.sharding import PartitionSpec as P

F32, BF16 = jnp.float32, jnp.bfloat16
TOK = 192
BACK = 9
KB = 576
ROWS = 1536
HEADS = 8
LOG2E = 1.4426950408889634
NEG = -1e30
SCALE2 = (128.0 ** -0.5) * LOG2E
PAY = 200
NT = (((1,), (1,)), ((), ()))
TN = (((0,), (0,)), ((), ()))


ORDER = ((8, 4, 0), (3, 2, 1), (7, 6, 5))


def keys_of(g):
    return pl.ds(pl.multiple_of(g * KB, KB), KB)


def load_window(where_ref, qdoc_ref, own_ref, recv_ref, kwin, vwin, ids_scr, start_scr, groups):
    block = where_ref[0]
    x = lax.rem(block, 4)
    ids_scr[...] = jnp.full_like(ids_scr, 100.0)
    lane = lax.broadcasted_iota(jnp.int32, (1, 256), 1)
    back = lax.broadcasted_iota(jnp.int32, (16, 1), 0)
    exists = jnp.zeros((16, 1), jnp.bool_)
    for g in groups:
        for b, k in enumerate(ORDER[g]):
            if k % 4 == 0:
                src = own_ref.at[k // 4]
            else:
                src = recv_ref.at[lax.rem(x - k + 8, 4), k // 4]
            row = g * 3 + b
            kwin[row * TOK:(row + 1) * TOK, :] = src[0:TOK, 0:128]
            if vwin is not None:
                vwin[row * TOK:(row + 1) * TOK, :] = src[0:TOK, 128:256]
            ids = src[TOK:TOK + 8, :].astype(F32)[0:1]
            ids_scr[row:row + 1, :] = jnp.where(lane < TOK, ids, 100.0)
            exists = exists | ((back == row) & (block >= k))
    ids = ids_scr[...]
    doc = qdoc_ref[...]
    start = jnp.zeros((16, ROWS), F32)
    for d in range(1, 4):
        count = jnp.sum(jnp.where(ids < d - 0.5, 1.0, 0.0), axis=1, keepdims=True)
        start = jnp.where(doc == d, count, start)
    start_scr[...] = jnp.where(exists, start, float(TOK)).astype(jnp.int32)


def masked_scores(key, q, start_scr, g, own):
    s = lax.dot_general(key, q, NT, preferred_element_type=F32) * SCALE2
    kp = lax.broadcasted_iota(jnp.int32, (TOK, ROWS), 0)
    parts = []
    for b in range(3):
        allowed = kp >= start_scr[pl.ds(g * 3 + b, 1), :]
        if own and b == 2:
            allowed = allowed & (kp <= lax.broadcasted_iota(jnp.int32, (1, ROWS), 1) // HEADS)
        parts.append(jnp.where(allowed, s[b * TOK:(b + 1) * TOK], NEG))
    return jnp.concatenate(parts)


def groups_used(start_scr):
    near = jnp.min(start_scr[5:6, :].astype(F32)) < TOK - 0.5
    far = jnp.min(start_scr[8:9, :].astype(F32)) < TOK - 0.5
    return 1 + near.astype(jnp.int32) + far.astype(jnp.int32)


def local_kernel(
    where_ref, qdoc_ref, q_ref, do_ref, o_ref, own_ref, t_ref, m_ref, l_ref, delta_ref, kwin, ids_scr, start_scr
):
    load_window(where_ref, qdoc_ref, own_ref, None, kwin, None, ids_scr, start_scr, (0,))
    t = masked_scores(kwin[...], q_ref[...], start_scr, 0, True)
    t_ref[...] = t
    t = t.reshape(KB // 8, 8, ROWS)
    top = jnp.max(t, axis=0)
    m_ref[...] = top
    l_ref[...] = jnp.sum(jnp.exp2(t - top), axis=0)
    delta_ref[...] = jnp.sum((do_ref[...].astype(F32) * o_ref[...].astype(F32)).T, axis=0, keepdims=True)


def key_value_kernel(
    where_ref, qdoc_ref, q_ref, do_ref, t_ref, m_ref, l_ref, delta_ref, own_ref, recv_ref,
    dkv_ref, stat_ref, kwin, vwin, t_scr, m_scr, l_scr, ids_scr, start_scr,
):
    load_window(where_ref, qdoc_ref, own_ref, recv_ref, kwin, vwin, ids_scr, start_scr, (0, 1, 2))
    used = groups_used(start_scr)
    m_scr[...] = m_ref[...]
    l_scr[...] = l_ref[...]

    def score_step(g, unused):
        t = masked_scores(kwin[keys_of(g), :], q_ref[...], start_scr, g, False)
        t_scr[keys_of(g - 1), :] = t
        t = t.reshape(KB // 8, 8, ROWS)
        old = m_scr[...]
        top = jnp.maximum(old, jnp.max(t, axis=0))
        m_scr[...] = top
        l_scr[...] = l_scr[...] * jnp.exp2(old - top) + jnp.sum(jnp.exp2(t - top), axis=0)
        return unused

    lax.fori_loop(1, used, score_step, 0)
    top = jnp.max(m_scr[...], axis=0, keepdims=True)
    total = jnp.sum(l_scr[...] * jnp.exp2(m_scr[...] - top), axis=0, keepdims=True)
    stat_ref[...] = top + jnp.log(total) * LOG2E

    def grad_step(g, t, blocks):
        q, do = q_ref[...], do_ref[...]
        prob = jnp.exp2(t - stat_ref[...])
        dp = lax.dot_general(vwin[keys_of(g), :], do, NT, preferred_element_type=F32)
        ds = (prob * (dp - delta_ref[...])).astype(BF16)
        dv = jnp.dot(prob.astype(BF16), do, preferred_element_type=F32)
        dk = jnp.dot(ds, q, preferred_element_type=F32)
        for b, back in enumerate(blocks):
            for r in range(4):
                part = slice(b * TOK + r * 48, b * TOK + r * 48 + 48)
                dkv_ref[r, back, :, 0:128] = dk[part].astype(BF16)
                dkv_ref[r, back, :, 128:256] = dv[part].astype(BF16)

    grad_step(0, t_ref[...], ORDER[0])

    def later_step(g, unused):
        grad_step(g, t_scr[keys_of(g - 1), :], [4 * g - 1 - b for b in range(3)])
        return unused

    lax.fori_loop(1, used, later_step, 0)

    def clear_step(g, unused):
        for b in range(3):
            for r in range(4):
                dkv_ref[r, 4 * g - 1 - b] = jnp.zeros((48, 256), BF16)
        return unused

    lax.fori_loop(used, 3, clear_step, 0)


def query_kernel(
    where_ref, qdoc_ref, q_ref, do_ref, stat_ref, delta_ref, own_ref, recv_ref,
    dq_ref, kwin, vwin, dq_acc, ids_scr, start_scr,
):
    load_window(where_ref, qdoc_ref, own_ref, recv_ref, kwin, vwin, ids_scr, start_scr, (0, 1, 2))

    def query_step(g, own):
        key = kwin[keys_of(g), :]
        prob = jnp.exp2(masked_scores(key, q_ref[...], start_scr, g, own) - stat_ref[...])
        dp = lax.dot_general(vwin[keys_of(g), :], do_ref[...], NT, preferred_element_type=F32)
        ds = (prob * (dp - delta_ref[...])).astype(BF16)
        return lax.dot_general(key, ds, TN, preferred_element_type=F32)

    dq_acc[...] = query_step(0, True)

    def later_step(g, unused):
        dq_acc[...] += query_step(g, False)
        return unused

    lax.fori_loop(1, groups_used(start_scr), later_step, 0)
    dq_ref[...] = (dq_acc[...].T * (128.0 ** -0.5)).astype(BF16)


VMEM_SPEC = pl.BlockSpec(memory_space=pltpu.VMEM)
SMEM_SPEC = pl.BlockSpec(memory_space=pltpu.SMEM)


def window_scratch():
    return [pltpu.VMEM((16, 256), F32), pltpu.VMEM((16, ROWS), jnp.int32)]


def local_scores(where, qdoc, q, do, o, own):
    return pl.pallas_call(
        local_kernel,
        out_shape=(
            jax.ShapeDtypeStruct((KB, ROWS), F32),
            jax.ShapeDtypeStruct((8, ROWS), F32),
            jax.ShapeDtypeStruct((8, ROWS), F32),
            jax.ShapeDtypeStruct((1, ROWS), F32),
        ),
        in_specs=[SMEM_SPEC] + [VMEM_SPEC] * 5,
        out_specs=(VMEM_SPEC,) * 4,
        scratch_shapes=[pltpu.VMEM((KB, 128), BF16)] + window_scratch(),
        compiler_params=pltpu.CompilerParams(vmem_limit_bytes=24 << 20),
        cost_estimate=pl.CostEstimate(flops=1 << 29, bytes_accessed=5 << 20, transcendentals=1 << 20),
    )(where, qdoc, q, do, o, own)


def key_value_grads(where, qdoc, q, do, local, own, recv):
    return pl.pallas_call(
        key_value_kernel,
        out_shape=(
            jax.ShapeDtypeStruct((4, BACK, 48, 256), BF16),
            jax.ShapeDtypeStruct((1, ROWS), F32),
        ),
        in_specs=[SMEM_SPEC] + [VMEM_SPEC] * 9,
        out_specs=(VMEM_SPEC, VMEM_SPEC),
        scratch_shapes=[
            pltpu.VMEM((BACK * TOK, 128), BF16),
            pltpu.VMEM((BACK * TOK, 128), BF16),
            pltpu.VMEM((2 * KB, ROWS), F32),
            pltpu.VMEM((8, ROWS), F32),
            pltpu.VMEM((8, ROWS), F32),
        ] + window_scratch(),
        compiler_params=pltpu.CompilerParams(vmem_limit_bytes=32 << 20),
        cost_estimate=pl.CostEstimate(flops=4 << 30, bytes_accessed=3 << 20, transcendentals=2 << 20),
    )(where, qdoc, q, do, *local, own, recv)


def query_grads(where, qdoc, q, do, stat, delta, own, recv):
    return pl.pallas_call(
        query_kernel,
        out_shape=jax.ShapeDtypeStruct((ROWS, 128), BF16),
        in_specs=[SMEM_SPEC] + [VMEM_SPEC] * 7,
        out_specs=VMEM_SPEC,
        scratch_shapes=[
            pltpu.VMEM((BACK * TOK, 128), BF16),
            pltpu.VMEM((BACK * TOK, 128), BF16),
            pltpu.VMEM((128, ROWS), F32),
        ] + window_scratch(),
        compiler_params=pltpu.CompilerParams(vmem_limit_bytes=32 << 20),
        cost_estimate=pl.CostEstimate(flops=3 << 30, bytes_accessed=3 << 20, transcendentals=2 << 20),
    )(where, qdoc, q, do, stat, delta, own, recv)


def attention_grads(where, qdoc, q, do, o, own, recv):
    local = local_scores(where, qdoc, q, do, o, own)
    recv, local = lax.optimization_barrier((recv, local))
    dkv, stat = key_value_grads(where, qdoc, q, do, local, own, recv)
    return query_grads(where, qdoc, q, do, stat, local[3], own, recv), dkv


def sum_kernel(group_ref, part_ref, out_ref):
    first = 4 * group_ref[0] - 8
    out_ref[...] = jnp.zeros_like(out_ref)
    for j in range(12):

        @pl.when(first + j >= 0)
        def _():
            terms = [part_ref[xs, 8 + xs - j].astype(F32) for xs in range(4) if 0 <= 8 + xs - j < BACK]
            out_ref[jnp.maximum(first + j, 0)] = sum(terms[1:], terms[0]).astype(BF16)


def sum_terms(group, part):
    return pl.pallas_call(
        sum_kernel,
        out_shape=jax.ShapeDtypeStruct((16, 48, 256), BF16),
        in_specs=[SMEM_SPEC, VMEM_SPEC],
        out_specs=VMEM_SPEC,
        compiler_params=pltpu.CompilerParams(vmem_limit_bytes=8 << 20),
        cost_estimate=pl.CostEstimate(flops=1 << 20, bytes_accessed=1 << 20, transcendentals=0),
    )(group, part)


def finish_kernel(last_ref, dk_ref, dv_ref):
    total = jnp.sum(last_ref[...].astype(F32), axis=0)
    dk_ref[...] = (total[:, 0:128] * (128.0 ** -0.5)).astype(BF16)
    dv_ref[...] = total[:, 128:256].astype(BF16)


def finish(last):
    return pl.pallas_call(
        finish_kernel,
        out_shape=(jax.ShapeDtypeStruct((48, 128), BF16),) * 2,
        in_specs=[VMEM_SPEC],
        out_specs=(VMEM_SPEC, VMEM_SPEC),
        compiler_params=pltpu.CompilerParams(vmem_limit_bytes=8 << 20),
        cost_estimate=pl.CostEstimate(flops=1 << 18, bytes_accessed=1 << 19, transcendentals=0),
    )(last)


X_GROUPS = [[4 * a + x for x in range(4)] for a in range(4)]


def on_device(queries, keys, values, doc_ids, output_gradient, attention_output):
    block = lax.axis_index("seq")
    a, x = block // 4, lax.rem(block, 4)
    tp = lax.axis_index("tp")
    core, half = tp % 2 == 1, tp >= 4
    near = ((tp // 2) % 2 == 1) != half
    bits = (half, near, core)

    def by_label(array):
        for axis, bit in enumerate(bits):
            array = jnp.where(bit, jnp.flip(array, axis), array)
        return array

    def relabel(array):
        return jnp.stack([array[0:2], jnp.flip(array[2:4], 0)])

    def by_core(array):
        return jnp.where(core, jnp.swapaxes(array, 0, 1), array)

    def swap(array, flip0, flip1):
        return lax.ppermute(array, "tp", [(i, i ^ (flip1 if i % 2 else flip0)) for i in range(8)])

    kv = jnp.concatenate([keys, values], axis=2).transpose(1, 0, 2).reshape(4, 2, 24, 256)
    part = by_label(relabel(kv))
    got = swap(part[:, :, 1], 1, 1)
    part = by_core(jnp.stack([part[:, :, 0], got], axis=2))
    got = swap(part[:, 1], 2, 6)
    part = jnp.stack([part[:, 0], got], axis=1)
    got = swap(part[1], 6, 2)
    part = by_label(by_core(jnp.stack([part[0], got])))
    kv = jnp.concatenate([part[0], jnp.flip(part[1], 0)]).reshape(TOK, 256)
    ids = jnp.pad(doc_ids.astype(BF16), (0, 64))
    tail = jnp.concatenate([ids[None], jnp.zeros((PAY - TOK - 1, 256), BF16)], axis=0)
    pay = jnp.concatenate([kv, tail], axis=0)
    back = [lax.ppermute(pay, "seq", [(i, i + k) for i in range(16 - k)]) for k in (4, 8)]
    own = jnp.stack([pay] + back)
    send = jnp.stack([jnp.where(x < dest, own[0:2], own[1:3]) for dest in range(4)])
    recv = lax.all_to_all(send, "seq", split_axis=0, concat_axis=0, tiled=True, axis_index_groups=X_GROUPS)
    qdoc = jnp.repeat(doc_ids, HEADS)[None]
    dq, dkv = attention_grads(
        block.reshape(1), qdoc,
        queries.reshape(ROWS, 128), output_gradient.reshape(ROWS, 128), attention_output.reshape(ROWS, 128),
        own, recv,
    )
    part = lax.all_to_all(dkv, "seq", split_axis=0, concat_axis=0, tiled=True, axis_index_groups=X_GROUPS)
    part, dq = lax.optimization_barrier((part, dq))
    last = lax.all_to_all(
        sum_terms(a.reshape(1), part), ("head", "seq"), split_axis=0, concat_axis=0, tiled=True,
        axis_index_groups=[[16 * h + 4 * z + xs for h in range(4) for z in range(4)] for xs in range(4)],
    )
    grad_keys, grad_values = finish(last)
    grad_keys, grad_values = grad_keys[:, None], grad_values[:, None]
    return dq.reshape(1, TOK, HEADS, 128), grad_keys, grad_values


def solution(mesh):
    placed = (
        P("head", "seq", "tp", None),
        P(("seq", "tp"), None, None),
        P(("seq", "tp"), None, None),
        P("seq"),
        P("head", "seq", "tp", None),
        P("head", "seq", "tp", None),
    )
    return jax.shard_map(
        on_device,
        mesh=mesh,
        in_specs=placed,
        out_specs=(
            P("head", "seq", "tp", None),
            P(("head", "seq"), "tp", None),
            P(("head", "seq"), "tp", None),
        ),
        check_vma=False,
    )
```

```python
import functools
import jax
import jax.numpy as jnp
from jax import lax
from jax.experimental import pallas as pl
from jax.experimental.pallas import tpu as pltpu
from jax.sharding import PartitionSpec as P

F32, BF16 = jnp.float32, jnp.bfloat16
TOK = 192
BACK = 9
KB = 576
ROWS = 1536
HEADS = 8
LOG2E = 1.4426950408889634
NEG = -1e30
SCALE2 = (128.0 ** -0.5) * LOG2E
PAY = 200
NT = (((1,), (1,)), ((), ()))
TN = (((0,), (0,)), ((), ()))


ORDER = ((8, 4, 0), (3, 2, 1), (7, 6, 5))


def keys_of(g):
    return pl.ds(pl.multiple_of(g * KB, KB), KB)


def load_window(where_ref, qdoc_ref, own_ref, recv_ref, kwin, vwin, ids_scr, start_scr, groups):
    block = where_ref[0]
    x = lax.rem(block, 4)
    ids_scr[...] = jnp.full_like(ids_scr, 100.0)
    lane = lax.broadcasted_iota(jnp.int32, (1, 256), 1)
    back = lax.broadcasted_iota(jnp.int32, (16, 1), 0)
    exists = jnp.zeros((16, 1), jnp.bool_)
    for g in groups:
        for b, k in enumerate(ORDER[g]):
            if k % 4 == 0:
                src = own_ref.at[k // 4]
            else:
                src = recv_ref.at[lax.rem(x - k + 8, 4), k // 4]
            row = g * 3 + b
            kwin[row * TOK:(row + 1) * TOK, :] = src[0:TOK, 0:128]
            if vwin is not None:
                vwin[row * TOK:(row + 1) * TOK, :] = src[0:TOK, 128:256]
            ids = src[TOK:TOK + 8, :].astype(F32)[0:1]
            ids_scr[row:row + 1, :] = jnp.where(lane < TOK, ids, 100.0)
            exists = exists | ((back == row) & (block >= k))
    ids = ids_scr[...]
    doc = qdoc_ref[...]
    start = jnp.zeros((16, ROWS), F32)
    for d in range(1, 4):
        count = jnp.sum(jnp.where(ids < d - 0.5, 1.0, 0.0), axis=1, keepdims=True)
        start = jnp.where(doc == d, count, start)
    start_scr[...] = jnp.where(exists, start, float(TOK)).astype(jnp.int32)


def masked_scores(key, q, start_scr, g, own):
    s = lax.dot_general(key, q, NT, preferred_element_type=F32) * SCALE2
    kp = lax.broadcasted_iota(jnp.int32, (TOK, ROWS), 0)
    parts = []
    for b in range(3):
        allowed = kp >= start_scr[pl.ds(g * 3 + b, 1), :]
        if own and b == 2:
            allowed = allowed & (kp <= lax.broadcasted_iota(jnp.int32, (1, ROWS), 1) // HEADS)
        parts.append(jnp.where(allowed, s[b * TOK:(b + 1) * TOK], NEG))
    return jnp.concatenate(parts)


def groups_used(start_scr):
    near = jnp.min(start_scr[5:6, :].astype(F32)) < TOK - 0.5
    far = jnp.min(start_scr[8:9, :].astype(F32)) < TOK - 0.5
    return 1 + near.astype(jnp.int32) + far.astype(jnp.int32)


def local_kernel(
    where_ref, qdoc_ref, q_ref, do_ref, o_ref, own_ref, m_ref, l_ref, delta_ref, kwin, ids_scr, start_scr
):
    load_window(where_ref, qdoc_ref, own_ref, None, kwin, None, ids_scr, start_scr, (0,))
    t = masked_scores(kwin[...], q_ref[...], start_scr, 0, True)
    t = t.reshape(KB // 8, 8, ROWS)
    top = jnp.max(t, axis=0)
    m_ref[...] = top
    l_ref[...] = jnp.sum(jnp.exp2(t - top), axis=0)
    delta_ref[...] = jnp.sum((do_ref[...].astype(F32) * o_ref[...].astype(F32)).T, axis=0, keepdims=True)


def key_value_kernel(
    where_ref, qdoc_ref, q_ref, do_ref, m_ref, l_ref, delta_ref, own_ref, recv_ref,
    dkv_ref, stat_ref, kwin, vwin, t_scr, m_scr, l_scr, ids_scr, start_scr,
):
    load_window(where_ref, qdoc_ref, own_ref, recv_ref, kwin, vwin, ids_scr, start_scr, (0, 1, 2))
    used = groups_used(start_scr)
    m_scr[...] = m_ref[...]
    l_scr[...] = l_ref[...]

    def score_step(g, unused):
        t = masked_scores(kwin[keys_of(g), :], q_ref[...], start_scr, g, False)
        t_scr[keys_of(g - 1), :] = t
        t = t.reshape(KB // 8, 8, ROWS)
        old = m_scr[...]
        top = jnp.maximum(old, jnp.max(t, axis=0))
        m_scr[...] = top
        l_scr[...] = l_scr[...] * jnp.exp2(old - top) + jnp.sum(jnp.exp2(t - top), axis=0)
        return unused

    lax.fori_loop(1, used, score_step, 0)
    top = jnp.max(m_scr[...], axis=0, keepdims=True)
    total = jnp.sum(l_scr[...] * jnp.exp2(m_scr[...] - top), axis=0, keepdims=True)
    stat_ref[...] = top + jnp.log(total) * LOG2E

    def grad_step(g, t, blocks):
        q, do = q_ref[...], do_ref[...]
        prob = jnp.exp2(t - stat_ref[...])
        dp = lax.dot_general(vwin[keys_of(g), :], do, NT, preferred_element_type=F32)
        ds = (prob * (dp - delta_ref[...])).astype(BF16)
        dv = jnp.dot(prob.astype(BF16), do, preferred_element_type=F32)
        dk = jnp.dot(ds, q, preferred_element_type=F32)
        for b, back in enumerate(blocks):
            for r in range(4):
                part = slice(b * TOK + r * 48, b * TOK + r * 48 + 48)
                dkv_ref[r, back, :, 0:128] = dk[part].astype(BF16)
                dkv_ref[r, back, :, 128:256] = dv[part].astype(BF16)

    grad_step(0, masked_scores(kwin[keys_of(0), :], q_ref[...], start_scr, 0, True), ORDER[0])

    def later_step(g, unused):
        grad_step(g, t_scr[keys_of(g - 1), :], [4 * g - 1 - b for b in range(3)])
        return unused

    lax.fori_loop(1, used, later_step, 0)

    def clear_step(g, unused):
        for b in range(3):
            for r in range(4):
                dkv_ref[r, 4 * g - 1 - b] = jnp.zeros((48, 256), BF16)
        return unused

    lax.fori_loop(used, 3, clear_step, 0)


def query_kernel(
    where_ref, qdoc_ref, q_ref, do_ref, stat_ref, delta_ref, own_ref, recv_ref,
    dq_ref, kwin, vwin, dq_acc, ids_scr, start_scr,
):
    load_window(where_ref, qdoc_ref, own_ref, recv_ref, kwin, vwin, ids_scr, start_scr, (0, 1, 2))

    def query_step(g, own):
        key = kwin[keys_of(g), :]
        prob = jnp.exp2(masked_scores(key, q_ref[...], start_scr, g, own) - stat_ref[...])
        dp = lax.dot_general(vwin[keys_of(g), :], do_ref[...], NT, preferred_element_type=F32)
        ds = (prob * (dp - delta_ref[...])).astype(BF16)
        return lax.dot_general(key, ds, TN, preferred_element_type=F32)

    dq_acc[...] = query_step(0, True)

    def later_step(g, unused):
        dq_acc[...] += query_step(g, False)
        return unused

    lax.fori_loop(1, groups_used(start_scr), later_step, 0)
    dq_ref[...] = (dq_acc[...].T * (128.0 ** -0.5)).astype(BF16)


VMEM_SPEC = pl.BlockSpec(memory_space=pltpu.VMEM)
SMEM_SPEC = pl.BlockSpec(memory_space=pltpu.SMEM)


def window_scratch():
    return [pltpu.VMEM((16, 256), F32), pltpu.VMEM((16, ROWS), jnp.int32)]


def local_scores(where, qdoc, q, do, o, own):
    return pl.pallas_call(
        local_kernel,
        out_shape=(
            jax.ShapeDtypeStruct((8, ROWS), F32),
            jax.ShapeDtypeStruct((8, ROWS), F32),
            jax.ShapeDtypeStruct((1, ROWS), F32),
        ),
        in_specs=[SMEM_SPEC] + [VMEM_SPEC] * 5,
        out_specs=(VMEM_SPEC,) * 3,
        scratch_shapes=[pltpu.VMEM((KB, 128), BF16)] + window_scratch(),
        compiler_params=pltpu.CompilerParams(vmem_limit_bytes=24 << 20),
        cost_estimate=pl.CostEstimate(flops=1 << 29, bytes_accessed=5 << 20, transcendentals=1 << 20),
    )(where, qdoc, q, do, o, own)


def key_value_grads(where, qdoc, q, do, local, own, recv):
    return pl.pallas_call(
        key_value_kernel,
        out_shape=(
            jax.ShapeDtypeStruct((4, BACK, 48, 256), BF16),
            jax.ShapeDtypeStruct((1, ROWS), F32),
        ),
        in_specs=[SMEM_SPEC] + [VMEM_SPEC] * 8,
        out_specs=(VMEM_SPEC, VMEM_SPEC),
        scratch_shapes=[
            pltpu.VMEM((BACK * TOK, 128), BF16),
            pltpu.VMEM((BACK * TOK, 128), BF16),
            pltpu.VMEM((2 * KB, ROWS), F32),
            pltpu.VMEM((8, ROWS), F32),
            pltpu.VMEM((8, ROWS), F32),
        ] + window_scratch(),
        compiler_params=pltpu.CompilerParams(vmem_limit_bytes=32 << 20),
        cost_estimate=pl.CostEstimate(flops=4 << 30, bytes_accessed=3 << 20, transcendentals=2 << 20),
    )(where, qdoc, q, do, *local, own, recv)


def query_grads(where, qdoc, q, do, stat, delta, own, recv):
    return pl.pallas_call(
        query_kernel,
        out_shape=jax.ShapeDtypeStruct((ROWS, 128), BF16),
        in_specs=[SMEM_SPEC] + [VMEM_SPEC] * 7,
        out_specs=VMEM_SPEC,
        scratch_shapes=[
            pltpu.VMEM((BACK * TOK, 128), BF16),
            pltpu.VMEM((BACK * TOK, 128), BF16),
            pltpu.VMEM((128, ROWS), F32),
        ] + window_scratch(),
        compiler_params=pltpu.CompilerParams(vmem_limit_bytes=32 << 20),
        cost_estimate=pl.CostEstimate(flops=3 << 30, bytes_accessed=3 << 20, transcendentals=2 << 20),
    )(where, qdoc, q, do, stat, delta, own, recv)


def attention_grads(where, qdoc, q, do, o, own, recv):
    local = local_scores(where, qdoc, q, do, o, own)
    recv, local = lax.optimization_barrier((recv, local))
    dkv, stat = key_value_grads(where, qdoc, q, do, local, own, recv)
    return query_grads(where, qdoc, q, do, stat, local[2], own, recv), dkv


def sum_kernel(group_ref, part_ref, out_ref):
    first = 4 * group_ref[0] - 8
    out_ref[...] = jnp.zeros_like(out_ref)
    for j in range(12):

        @pl.when(first + j >= 0)
        def _():
            terms = [part_ref[xs, 8 + xs - j].astype(F32) for xs in range(4) if 0 <= 8 + xs - j < BACK]
            out_ref[jnp.maximum(first + j, 0)] = sum(terms[1:], terms[0]).astype(BF16)


def sum_terms(group, part):
    return pl.pallas_call(
        sum_kernel,
        out_shape=jax.ShapeDtypeStruct((16, 48, 256), BF16),
        in_specs=[SMEM_SPEC, VMEM_SPEC],
        out_specs=VMEM_SPEC,
        compiler_params=pltpu.CompilerParams(vmem_limit_bytes=8 << 20),
        cost_estimate=pl.CostEstimate(flops=1 << 20, bytes_accessed=1 << 20, transcendentals=0),
    )(group, part)


def finish_kernel(last_ref, dk_ref, dv_ref):
    total = jnp.sum(last_ref[...].astype(F32), axis=0)
    dk_ref[...] = (total[:, 0:128] * (128.0 ** -0.5)).astype(BF16)
    dv_ref[...] = total[:, 128:256].astype(BF16)


def finish(last):
    return pl.pallas_call(
        finish_kernel,
        out_shape=(jax.ShapeDtypeStruct((48, 128), BF16),) * 2,
        in_specs=[VMEM_SPEC],
        out_specs=(VMEM_SPEC, VMEM_SPEC),
        compiler_params=pltpu.CompilerParams(vmem_limit_bytes=8 << 20),
        cost_estimate=pl.CostEstimate(flops=1 << 18, bytes_accessed=1 << 19, transcendentals=0),
    )(last)


X_GROUPS = [[4 * a + x for x in range(4)] for a in range(4)]


def on_device(queries, keys, values, doc_ids, output_gradient, attention_output):
    block = lax.axis_index("seq")
    a, x = block // 4, lax.rem(block, 4)
    tp = lax.axis_index("tp")
    core, half = tp % 2 == 1, tp >= 4
    near = ((tp // 2) % 2 == 1) != half
    bits = (half, near, core)

    def by_label(array):
        for axis, bit in enumerate(bits):
            array = jnp.where(bit, jnp.flip(array, axis), array)
        return array

    def relabel(array):
        return jnp.stack([array[0:2], jnp.flip(array[2:4], 0)])

    def by_core(array):
        return jnp.where(core, jnp.swapaxes(array, 0, 1), array)

    def swap(array, flip0, flip1):
        return lax.ppermute(array, "tp", [(i, i ^ (flip1 if i % 2 else flip0)) for i in range(8)])

    kv = jnp.concatenate([keys, values], axis=2).transpose(1, 0, 2).reshape(4, 2, 24, 256)
    part = by_label(relabel(kv))
    got = swap(part[:, :, 1], 1, 1)
    part = by_core(jnp.stack([part[:, :, 0], got], axis=2))
    got = swap(part[:, 1], 2, 6)
    part = jnp.stack([part[:, 0], got], axis=1)
    got = swap(part[1], 6, 2)
    part = by_label(by_core(jnp.stack([part[0], got])))
    kv = jnp.concatenate([part[0], jnp.flip(part[1], 0)]).reshape(TOK, 256)
    ids = jnp.pad(doc_ids.astype(BF16), (0, 64))
    tail = jnp.concatenate([ids[None], jnp.zeros((PAY - TOK - 1, 256), BF16)], axis=0)
    pay = jnp.concatenate([kv, tail], axis=0)
    back = [lax.ppermute(pay, "seq", [(i, i + k) for i in range(16 - k)]) for k in (4, 8)]
    own = jnp.stack([pay] + back)
    send = jnp.stack([jnp.where(x < dest, own[0:2], own[1:3]) for dest in range(4)])
    recv = lax.all_to_all(send, "seq", split_axis=0, concat_axis=0, tiled=True, axis_index_groups=X_GROUPS)
    qdoc = jnp.repeat(doc_ids, HEADS)[None]
    dq, dkv = attention_grads(
        block.reshape(1), qdoc,
        queries.reshape(ROWS, 128), output_gradient.reshape(ROWS, 128), attention_output.reshape(ROWS, 128),
        own, recv,
    )
    part = lax.all_to_all(dkv, "seq", split_axis=0, concat_axis=0, tiled=True, axis_index_groups=X_GROUPS)
    part, dq = lax.optimization_barrier((part, dq))
    last = lax.all_to_all(
        sum_terms(a.reshape(1), part), ("head", "seq"), split_axis=0, concat_axis=0, tiled=True,
        axis_index_groups=[[16 * h + 4 * z + xs for h in range(4) for z in range(4)] for xs in range(4)],
    )
    grad_keys, grad_values = finish(last)
    grad_keys, grad_values = grad_keys[:, None], grad_values[:, None]
    return dq.reshape(1, TOK, HEADS, 128), grad_keys, grad_values


def solution(mesh):
    placed = (
        P("head", "seq", "tp", None),
        P(("seq", "tp"), None, None),
        P(("seq", "tp"), None, None),
        P("seq"),
        P("head", "seq", "tp", None),
        P("head", "seq", "tp", None),
    )
    return jax.shard_map(
        on_device,
        mesh=mesh,
        in_specs=placed,
        out_specs=(
            P("head", "seq", "tp", None),
            P(("head", "seq"), "tp", None),
            P(("head", "seq"), "tp", None),
        ),
        check_vma=False,
    )
```
